32 devices in a mesh: ctx: 8 (over y, x, core), head: 4 (over z).
Axes of the slice: x: 2, y: 2, z: 4, core: 2. Of those that a mesh axis runs over, the one named last changes fastest.
Arguments:
- queries: bfloat16 [640, 8192], P(('ctx', 'head')), may hold values from -18 to 18
- keys: bfloat16 [640, 1024], P(('ctx', 'head')), may hold values from -4.5 to 4.5
- values: bfloat16 [640, 1024], P(('ctx', 'head')), may hold values from -12 to 12
- block_order: int32 [16], replicated, may hold values from 0 to 15, each once
Outputs:
- attended: bfloat16 [640, 8192], P(('ctx', 'head'))
The draws below stay inside these ranges and needn't reach their ends.
Inputs may be any that keep to these rules, and one draw needn't show every extreme that they name: Storage block b holds sequence block block_order[b], its tokens in order; block_order is a permutation.
All inputs are finite; a program needn't handle non-finite values.
Results may differ from the reference program's by a relative error of at most 0.0049.
Values may be sent and summed in bfloat16 or wider, within the bound.
A program may use at most 64 MiB of HBM per device.

```python
import jax
import jax.numpy as jnp
from jax import lax

QUERY_HEADS = 64
VALUE_KEY_HEADS = 8
HEAD_DIMENSION = 128
BLOCK_TOKENS = 40
SEQUENCE_TOKENS = 640
NBLK = 16


def key_base(key):
    key_start_offset = jax.random.fold_in(key, 7)
    return jnp.clip(jax.random.normal(key_start_offset, (SEQUENCE_TOKENS, VALUE_KEY_HEADS, HEAD_DIMENSION), jnp.float32), -4.0, 4.0)


def draw_keys(key, part):
    lookup_rows = key_base(key)
    return lookup_rows.reshape(SEQUENCE_TOKENS, VALUE_KEY_HEADS * HEAD_DIMENSION).astype(jnp.bfloat16)


def draw_queries(key, part):
    query_key = jax.random.fold_in(key, 23)
    start_offset = 2.0 * jnp.clip(jax.random.normal(query_key, (SEQUENCE_TOKENS, QUERY_HEADS, HEAD_DIMENSION), jnp.float32), -5.0, 5.0)
    return start_offset.reshape(SEQUENCE_TOKENS, QUERY_HEADS * HEAD_DIMENSION).astype(jnp.bfloat16)


def block_scale(stream_key, dims, shards, smallest, top_value):
    def one(dim, shards_of):
        draws = jax.random.uniform(jax.random.fold_in(jax.random.fold_in(stream_key, 6), dim), (shards_of,), jnp.float32, smallest / len(shards), top_value / len(shards))
        return jnp.repeat(jnp.exp(draws), dims[dim] // shards_of).reshape((-1,) + (1,) * (len(dims) - dim - 1))

    factor_of = one(*shards[0])
    for cut in shards[1:]:
        factor_of = factor_of * one(*cut)
    return factor_of


def noise(key, extent, deviation, reach, cuts=(), kind=jnp.bfloat16):
    drawn = jax.random.normal(key, extent, jnp.float32) * deviation
    if len(cuts) > 0:
        drawn = block_scale(key, extent, cuts, -0.22, 0.18) * drawn
    return jnp.clip(drawn, min=-reach, max=reach).astype(kind)


def setup_inputs(seed: int = 0) -> dict:
    key_list = jax.random.split(jax.random.key(seed), 5)
    return {
        "queries": draw_queries(jax.random.fold_in(key_list[4], 71), 0),
        "keys": draw_keys(jax.random.fold_in(key_list[4], 71), 0),
        "values": noise(key_list[2], (SEQUENCE_TOKENS, VALUE_KEY_HEADS * HEAD_DIMENSION), 3.0, 12.0, ((0, 32),)),
        "block_order": jax.random.permutation(key_list[3], NBLK).astype(jnp.int32),
    }


def reference(queries, keys, values, block_order):
    row_ids = jnp.arange(SEQUENCE_TOKENS, dtype=jnp.int32)
    token_pos = block_order[row_ids // BLOCK_TOKENS] * BLOCK_TOKENS + row_ids % BLOCK_TOKENS
    heads_per_group = QUERY_HEADS // VALUE_KEY_HEADS
    score_scale = HEAD_DIMENSION ** -0.5
    key_lookup_rows = keys.reshape(SEQUENCE_TOKENS, VALUE_KEY_HEADS, HEAD_DIMENSION).astype(jnp.float32)
    value_lookup_rows = values.reshape(SEQUENCE_TOKENS, VALUE_KEY_HEADS, HEAD_DIMENSION).astype(jnp.float32)
    query_block_list = queries.reshape(SEQUENCE_TOKENS // BLOCK_TOKENS, BLOCK_TOKENS, VALUE_KEY_HEADS, heads_per_group, HEAD_DIMENSION)
    pos_blocks = token_pos.reshape(SEQUENCE_TOKENS // BLOCK_TOKENS, BLOCK_TOKENS)

    def one_block(block_item):
        query_block, query_pos = block_item
        scores = jnp.einsum("qkgd,nkd->kgqn", query_block.astype(jnp.float32), key_lookup_rows) * score_scale
        visible = token_pos[None, :] <= query_pos[:, None]
        scores = jnp.where(visible[None, None], scores, -jnp.inf)
        row_max = jnp.max(scores, axis=3, keepdims=True)
        raw_weights = jnp.exp(scores - row_max)
        denominator = jnp.sum(raw_weights, axis=3)
        weights = lax.optimization_barrier(raw_weights.astype(jnp.bfloat16)).astype(jnp.float32)
        numerator = jnp.einsum("kgqn,nkd->qkgd", weights, value_lookup_rows)
        return (numerator / jnp.transpose(denominator, (2, 0, 1))[..., None]).astype(jnp.bfloat16)

    attended = lax.map(one_block, (query_block_list, pos_blocks))
    return attended.reshape(SEQUENCE_TOKENS, QUERY_HEADS * HEAD_DIMENSION)
```

```python
import functools
import math

import jax
import jax.numpy as jnp
import numpy as np
from jax import lax
from jax.experimental import pallas as pl
from jax.experimental.pallas import tpu as pltpu
from jax.sharding import PartitionSpec as P

QUERY_HEADS = 64
VALUE_KEY_HEADS = 8
HEAD_DIMENSION = 128


def token_positions(block_order, row_ids, block_rows):
    block_ids = row_ids // block_rows
    block_table = jnp.arange(block_order.shape[0], dtype=jnp.int32)
    chosen = jnp.sum(
        jnp.where(block_ids[:, None] == block_table[None, :], block_order[None, :], 0), axis=1
    )
    return chosen * block_rows + row_ids % block_rows


def attend(states, query_block, query_pos, key_rows, value_rows, key_pos, key_heads, score_scale):
    max_old, total_old, weighted_old = states
    query_count = query_block.shape[0]
    head_size = key_rows.shape[1] // key_heads
    heads_per_group = query_block.shape[1] // (key_heads * head_size)
    head_total = key_heads * heads_per_group
    query_split = query_block.reshape(query_count, key_heads, heads_per_group, head_size)
    key_split = key_rows.reshape(-1, key_heads, head_size)
    value_split = value_rows.reshape(-1, key_heads, head_size)
    scores = (
        jnp.einsum("qkgd,nkd->kgqn", query_split, key_split, preferred_element_type=jnp.float32)
        * score_scale
    )
    visible = key_pos[None, :] <= query_pos[:, None]
    scores = jnp.where(visible[None, None], scores, -jnp.inf)
    max_prev = max_old.reshape(key_heads, heads_per_group, query_count)
    max_new = jnp.maximum(max_prev, jnp.max(scores, axis=3))
    weights = jnp.exp(scores - max_new[..., None])
    rescale = jnp.exp(max_prev - max_new)
    total_new = total_old.reshape(key_heads, heads_per_group, query_count) * rescale + jnp.sum(
        weights, axis=3
    )
    mixed_values = jnp.einsum(
        "kgqn,nkd->qkgd",
        weights.astype(jnp.bfloat16),
        value_split,
        preferred_element_type=jnp.float32,
    )
    weighted_new = (
        weighted_old.reshape(query_count, key_heads, heads_per_group, head_size)
        * jnp.transpose(rescale, (2, 0, 1))[..., None]
        + mixed_values
    )
    return (
        max_new.reshape(head_total, query_count),
        total_new.reshape(head_total, query_count),
        weighted_new.reshape(query_count, head_total * head_size),
    )


def on_device(queries, keys, values, block_order):
    head_count = lax.axis_size("head")
    ctx_index = lax.axis_index("ctx")
    tokens_per_shard = queries.shape[0]
    query_heads = QUERY_HEADS // head_count
    heads_per_group = QUERY_HEADS // VALUE_KEY_HEADS
    local_kv = max(1, query_heads // heads_per_group)
    score_scale = HEAD_DIMENSION ** (-0.5)
    placement_index = np.array(
        [
            slot_number * query_heads // heads_per_group + offset
            for slot_number in range(head_count)
            for offset in range(local_kv)
        ],
        dtype=np.int32,
    )
    key_placements = keys.reshape(tokens_per_shard, VALUE_KEY_HEADS, HEAD_DIMENSION)[
        :, placement_index, :
    ].reshape(tokens_per_shard, head_count * local_kv * HEAD_DIMENSION)
    value_placements = values.reshape(tokens_per_shard, VALUE_KEY_HEADS, HEAD_DIMENSION)[
        :, placement_index, :
    ].reshape(tokens_per_shard, head_count * local_kv * HEAD_DIMENSION)
    tok_ctx = tokens_per_shard * head_count
    block_rows = tok_ctx // 2
    query_pos = token_positions(
        block_order, ctx_index * tok_ctx + jnp.arange(tok_ctx, dtype=jnp.int32), block_rows
    )

    def make_fold(query_all, key_heads, position_of):

        def tile(states, key_rows, value_rows, key_pos):
            updated = []
            for number in range(2):
                query_block = query_all[number * block_rows : (number + 1) * block_rows]
                block_pos = query_pos[number * block_rows : (number + 1) * block_rows]
                reach = jnp.min(key_pos) <= jnp.max(block_pos)
                updated.append(
                    lax.cond(
                        reach,
                        lambda carry_state: attend(
                            carry_state,
                            query_block,
                            block_pos,
                            key_rows,
                            value_rows,
                            key_pos,
                            key_heads,
                            score_scale,
                        ),
                        lambda carry_state: carry_state,
                        states[number],
                    )
                )
            return tuple(updated)

        def fold_step(states, key_piece, first_row):
            key_rows, value_rows = key_piece
            count = key_rows.shape[0]
            key_pos = position_of(jnp.arange(count, dtype=jnp.int32))
            piece_rows = tok_ctx * math.gcd(count // tok_ctx, 4)
            splits = count // piece_rows

            def scan_step(carry_states, parts):
                return (tile(carry_states, parts[0], parts[1], parts[2]), None)

            states, unused = lax.scan(
                scan_step,
                states,
                (
                    key_rows.reshape(splits, piece_rows, -1),
                    value_rows.reshape(splits, piece_rows, -1),
                    key_pos.reshape(splits, piece_rows),
                ),
            )
            return states

        return fold_step

    local_q, local_k, local_v = (
        lax.all_to_all(queries, "head", split_axis=1, concat_axis=0, tiled=True),
        lax.all_to_all(key_placements, "head", split_axis=1, concat_axis=0, tiled=True),
        lax.all_to_all(value_placements, "head", split_axis=1, concat_axis=0, tiled=True),
    )

    def full_positions(row_ids):
        return token_positions(block_order, row_ids, block_rows)

    fold_each = make_fold(local_q, local_kv, full_positions)
    one_state = (
        jnp.full((query_heads, block_rows), -1e30, jnp.float32),
        jnp.zeros((query_heads, block_rows), jnp.float32),
        jnp.zeros((block_rows, query_heads * HEAD_DIMENSION), jnp.float32),
    )
    states = fold_each(
        (one_state, one_state),
        (
            lax.all_gather(local_k, "ctx", axis=0, tiled=True),
            lax.all_gather(local_v, "ctx", axis=0, tiled=True),
        ),
        jnp.int32(0),
    )
    total_all = jnp.concatenate([states[0][1], states[1][1]], axis=1)
    weighted_all = jnp.concatenate([states[0][2], states[1][2]], axis=0)
    weighted_all = weighted_all.reshape(tok_ctx, query_heads, HEAD_DIMENSION)
    attended = (
        (weighted_all / total_all.T[:, :, None])
        .reshape(tok_ctx, query_heads * HEAD_DIMENSION)
        .astype(jnp.bfloat16)
    )
    return lax.all_to_all(attended, "head", split_axis=0, concat_axis=1, tiled=True)


ROWS = 20
MAIN = 16
REST = ROWS - MAIN
GROUP = QUERY_HEADS // VALUE_KEY_HEADS
HALF = VALUE_KEY_HEADS * ROWS
ZS = 4
SLOTS = 8 * ZS
Z_ORDER = (1, 3, 2)


def slot_of(core, place, z):
    return (core * 4 + place) * ZS + z


def copy_names():
    names = [("z", r) for r in range(1, ZS)]
    for kind in ("x", "y", "dx", "dy", "m0", "m1", "m2", "mk", "mv"):
        names += [(kind, r) for r in range(ZS)]
    return names


NAMES = copy_names()


def gather_attend(
    block_rows, order_ref, q_ref, k_ref, v_ref, o_ref,
    q_in, q_all, q_rest, own_rest, chunks, k_rest, v_rest, bias, q_sem, send_sem, recv_sem,
):
    ctx, z = lax.axis_index("ctx"), lax.axis_index("head")
    bits = (lax.rem(ctx, 2), lax.rem(lax.div(ctx, 2), 2), lax.div(ctx, 4))
    mate = (ctx + 1 - 2 * bits[0], z)
    x_next = (ctx + 2 - 4 * bits[1], z)
    y_next = (ctx + 4 - 8 * bits[2], z)
    z_to = {r: (ctx, lax.rem(z + ZS - r, ZS)) for r in range(1, ZS)}

    barrier = pltpu.get_barrier_semaphore()
    partners = [mate, x_next, y_next] + [z_to[r] for r in range(1, ZS)]
    for partner in partners:
        pl.semaphore_signal(
            barrier, inc=1, device_id=partner, device_id_type=pl.DeviceIdType.MESH
        )
    q_copy = pltpu.make_async_copy(q_ref, q_in, q_sem)
    q_copy.start()

    for which, ref in enumerate((k_ref, v_ref)):
        base = which * HALF
        for h in range(VALUE_KEY_HEADS):
            lanes = slice(h * HEAD_DIMENSION, (h + 1) * HEAD_DIMENSION)
            chunks[0, base + h * MAIN : base + (h + 1) * MAIN, :] = ref[0:MAIN, lanes]
            own_rest[which, h * REST : (h + 1) * REST, :] = ref[MAIN:ROWS, lanes].astype(
                jnp.float32
            )
        chunks[0, base + VALUE_KEY_HEADS * MAIN : base + HALF, :] = own_rest[which].astype(
            jnp.bfloat16
        )

    ids = {name: number for number, name in enumerate(NAMES)}

    def part(slot, half):
        if half is None:
            return chunks.at[slot]
        return chunks.at[slot, half * HALF : (half + 1) * HALF]

    def copy(name):
        kind, r = name
        target, source, sink, half = {
            "z": (z_to.get(r), slot_of(0, 0, 0), slot_of(0, 0, r), None),
            "x": (x_next, slot_of(0, 0, r), slot_of(0, 1, r), None),
            "y": (y_next, slot_of(0, 0, r), slot_of(0, 2, r), None),
            "dx": (x_next, slot_of(0, 2, r), slot_of(0, 3, r), 1),
            "dy": (y_next, slot_of(0, 1, r), slot_of(0, 3, r), 0),
            "m0": (mate, slot_of(0, 0, r), slot_of(1, 0, r), None),
            "m1": (mate, slot_of(0, 1, r), slot_of(1, 1, r), None),
            "m2": (mate, slot_of(0, 2, r), slot_of(1, 2, r), None),
            "mk": (mate, slot_of(0, 3, r), slot_of(1, 3, r), 0),
            "mv": (mate, slot_of(0, 3, r), slot_of(1, 3, r), 1),
        }[kind]
        return pltpu.make_async_remote_copy(
            src_ref=part(source, half),
            dst_ref=part(sink, half),
            send_sem=send_sem.at[ids[name]],
            recv_sem=recv_sem.at[ids[name]],
            device_id=target,
            device_id_type=pl.DeviceIdType.MESH,
        )

    copies = {name: copy(name) for name in NAMES}

    def rest_rows(slot):
        for which, sink in ((0, k_rest), (1, v_rest)):
            top = which * HALF + VALUE_KEY_HEADS * MAIN
            rows = chunks[slot, top : top + VALUE_KEY_HEADS * REST, :].astype(jnp.float32)
            for h in range(VALUE_KEY_HEADS):
                sink[h, slot * REST : (slot + 1) * REST, :] = rows[h * REST : (h + 1) * REST]

    def arrived(*name):
        copies[name].wait_recv()

    def start(*name):
        copies[name].start()

    pl.semaphore_wait(barrier, len(partners))
    for r in Z_ORDER:
        start("z", r)
    start("x", 0)
    start("y", 0)
    start("m0", 0)

    lane = lax.broadcasted_iota(jnp.int32, (8, SLOTS * ROWS), 1)
    late = lane >= SLOTS * MAIN
    lane_slot = jnp.where(late, lax.div(lane - SLOTS * MAIN, REST), lax.div(lane, MAIN))
    lane_token = jnp.where(late, MAIN + lax.rem(lane, REST), lax.rem(lane, MAIN))
    key_pos = lane_token

    def first_position(flips, r):
        other = 0
        for number, flip in enumerate(flips):
            bit = 1 - bits[number] if flip else bits[number]
            other = other + bit * (1 << number)
        row = (other * ZS + lax.rem(z + r, ZS)) * ROWS
        return order_ref[lax.div(row, block_rows)] * block_rows + lax.rem(row, block_rows)

    for core in range(2):
        for place in range(4):
            for r in range(ZS):
                at = first_position((core, place % 2, place // 2), r)
                key_pos = key_pos + jnp.where(lane_slot == slot_of(core, place, r), at, 0)
    row = lax.broadcasted_iota(jnp.int32, (HALF, SLOTS * ROWS), 0)
    row_token = jnp.where(row >= GROUP * MAIN, MAIN + lax.rem(row, REST), lax.rem(row, MAIN))
    visible = key_pos[0:1, :] - first_position((0, 0, 0), 0) <= row_token
    bias[...] = jnp.where(visible, 0.0, -jnp.inf)

    q_copy.wait()
    for h in range(VALUE_KEY_HEADS):
        for g in range(GROUP):
            lanes = slice((h * GROUP + g) * HEAD_DIMENSION, (h * GROUP + g + 1) * HEAD_DIMENSION)
            q_all[h, g * MAIN : (g + 1) * MAIN, :] = q_in[0:MAIN, lanes]
            q_rest[h, g * REST : (g + 1) * REST, :] = q_in[MAIN:ROWS, lanes].astype(jnp.float32)
        q_all[h, GROUP * MAIN : HALF, :] = q_rest[h].astype(jnp.bfloat16)
    rest_rows(0)

    def pass_first(r):
        arrived("z", r)
        start("x", r)
        start("y", r)
        start("m0", r)
        rest_rows(slot_of(0, 0, r))

    def pass_second(r):
        arrived("x", r)
        start("dy", r)
        start("m1", r)
        arrived("y", r)
        start("dx", r)
        start("m2", r)
        rest_rows(slot_of(0, 1, r))
        rest_rows(slot_of(0, 2, r))

    def pass_third(r):
        arrived("dy", r)
        start("mk", r)
        arrived("dx", r)
        start("mv", r)
        rest_rows(slot_of(0, 3, r))
        for place in range(3):
            arrived("m%d" % place, r)
            rest_rows(slot_of(1, place, r))

    pass_second(0)
    for r in Z_ORDER:
        pass_first(r)
    pass_third(0)
    for r in Z_ORDER:
        pass_second(r)
    for r in Z_ORDER:
        pass_third(r)
    for r in (0,) + Z_ORDER:
        arrived("mk", r)
        arrived("mv", r)
        rest_rows(slot_of(1, 3, r))

    scale = HEAD_DIMENSION ** (-0.5)
    whole = (((1,), (1,)), ((), ()))
    for h in range(VALUE_KEY_HEADS):
        rows = slice(h * MAIN, (h + 1) * MAIN)
        queries = q_all[h]
        keys = chunks[:, rows, :].reshape(SLOTS * MAIN, HEAD_DIMENSION)
        values = chunks[:, HALF + h * MAIN : HALF + (h + 1) * MAIN, :].reshape(
            SLOTS * MAIN, HEAD_DIMENSION
        )
        scores = jnp.concatenate(
            [
                lax.dot_general(queries, keys, whole, preferred_element_type=jnp.float32),
                lax.dot_general(
                    queries,
                    k_rest[h].astype(jnp.bfloat16),
                    whole,
                    preferred_element_type=jnp.float32,
                ),
            ],
            axis=1,
        ) + bias[...]
        top = jnp.max(scores, axis=1, keepdims=True)
        weights = jnp.exp((scores - top) * scale)
        total = jnp.sum(weights, axis=1, keepdims=True)
        weights = weights.astype(jnp.bfloat16)
        mixed = jnp.dot(
            weights[:, : SLOTS * MAIN], values, preferred_element_type=jnp.float32
        ) + jnp.dot(
            weights[:, SLOTS * MAIN :],
            v_rest[h].astype(jnp.bfloat16),
            preferred_element_type=jnp.float32,
        )
        mixed = mixed / total
        for g in range(GROUP):
            lanes = slice((h * GROUP + g) * HEAD_DIMENSION, (h * GROUP + g + 1) * HEAD_DIMENSION)
            o_ref[0:MAIN, lanes] = mixed[g * MAIN : (g + 1) * MAIN].astype(jnp.bfloat16)
            first = GROUP * MAIN + g * REST
            o_ref[MAIN:ROWS, lanes] = mixed[first : first + REST].astype(jnp.bfloat16)

    for name in NAMES:
        copies[name].wait_send()


def on_device_gathered(queries, keys, values, block_order):
    block_rows = queries.shape[0] * lax.axis_size("ctx") * lax.axis_size("head")
    block_rows = block_rows // block_order.shape[0]
    bf16, f32 = jnp.bfloat16, jnp.float32
    in_vmem = pl.BlockSpec(memory_space=pltpu.VMEM)
    return pl.pallas_call(
        functools.partial(gather_attend, block_rows),
        out_shape=jax.ShapeDtypeStruct(queries.shape, bf16),
        in_specs=[
            pl.BlockSpec(memory_space=pltpu.SMEM),
            pl.BlockSpec(memory_space=pl.ANY),
            in_vmem,
            in_vmem,
        ],
        out_specs=in_vmem,
        scratch_shapes=[
            pltpu.VMEM(queries.shape, bf16),
            pltpu.VMEM((VALUE_KEY_HEADS, HALF, HEAD_DIMENSION), bf16),
            pltpu.VMEM((VALUE_KEY_HEADS, GROUP * REST, HEAD_DIMENSION), f32),
            pltpu.VMEM((2, VALUE_KEY_HEADS * REST, HEAD_DIMENSION), f32),
            pltpu.VMEM((SLOTS, 2 * HALF, HEAD_DIMENSION), bf16),
            pltpu.VMEM((VALUE_KEY_HEADS, SLOTS * REST, HEAD_DIMENSION), f32),
            pltpu.VMEM((VALUE_KEY_HEADS, SLOTS * REST, HEAD_DIMENSION), f32),
            pltpu.VMEM((HALF, SLOTS * ROWS), f32),
            pltpu.SemaphoreType.DMA,
            pltpu.SemaphoreType.DMA((len(NAMES),)),
            pltpu.SemaphoreType.DMA((len(NAMES),)),
        ],
        compiler_params=pltpu.CompilerParams(
            collective_id=0, has_side_effects=True, vmem_limit_bytes=32 * 1024 * 1024
        ),
    )(block_order, queries, keys, values)


def gathers_whole(mesh, queries, block_order):
    if mesh.shape["ctx"] != 8 or mesh.shape["head"] != ZS:
        return False
    rows = queries.shape[0]
    return rows == SLOTS * ROWS and (rows // block_order.shape[0]) % ROWS == 0


def solution(mesh):
    placed = (P(("ctx", "head"), None), P(("ctx", "head"), None), P(("ctx", "head"), None), P())

    def run(queries, keys, values, block_order):
        body = on_device_gathered if gathers_whole(mesh, queries, block_order) else on_device
        return jax.shard_map(
            body, mesh=mesh, in_specs=placed, out_specs=P(("ctx", "head"), None), check_vma=False
        )(queries, keys, values, block_order)

    return run
```

```python
import functools
import math

import jax
import jax.numpy as jnp
import numpy as np
from jax import lax
from jax.experimental import pallas as pl
from jax.experimental.pallas import tpu as pltpu
from jax.sharding import PartitionSpec as P

QUERY_HEADS = 64
VALUE_KEY_HEADS = 8
HEAD_DIMENSION = 128


def token_positions(block_order, row_ids, block_rows):
    block_ids = row_ids // block_rows
    block_table = jnp.arange(block_order.shape[0], dtype=jnp.int32)
    chosen = jnp.sum(
        jnp.where(block_ids[:, None] == block_table[None, :], block_order[None, :], 0), axis=1
    )
    return chosen * block_rows + row_ids % block_rows


def attend(states, query_block, query_pos, key_rows, value_rows, key_pos, key_heads, score_scale):
    max_old, total_old, weighted_old = states
    query_count = query_block.shape[0]
    head_size = key_rows.shape[1] // key_heads
    heads_per_group = query_block.shape[1] // (key_heads * head_size)
    head_total = key_heads * heads_per_group
    query_split = query_block.reshape(query_count, key_heads, heads_per_group, head_size)
    key_split = key_rows.reshape(-1, key_heads, head_size)
    value_split = value_rows.reshape(-1, key_heads, head_size)
    scores = (
        jnp.einsum("qkgd,nkd->kgqn", query_split, key_split, preferred_element_type=jnp.float32)
        * score_scale
    )
    visible = key_pos[None, :] <= query_pos[:, None]
    scores = jnp.where(visible[None, None], scores, -jnp.inf)
    max_prev = max_old.reshape(key_heads, heads_per_group, query_count)
    max_new = jnp.maximum(max_prev, jnp.max(scores, axis=3))
    weights = jnp.exp(scores - max_new[..., None])
    rescale = jnp.exp(max_prev - max_new)
    total_new = total_old.reshape(key_heads, heads_per_group, query_count) * rescale + jnp.sum(
        weights, axis=3
    )
    mixed_values = jnp.einsum(
        "kgqn,nkd->qkgd",
        weights.astype(jnp.bfloat16),
        value_split,
        preferred_element_type=jnp.float32,
    )
    weighted_new = (
        weighted_old.reshape(query_count, key_heads, heads_per_group, head_size)
        * jnp.transpose(rescale, (2, 0, 1))[..., None]
        + mixed_values
    )
    return (
        max_new.reshape(head_total, query_count),
        total_new.reshape(head_total, query_count),
        weighted_new.reshape(query_count, head_total * head_size),
    )


def on_device(queries, keys, values, block_order):
    head_count = lax.axis_size("head")
    ctx_index = lax.axis_index("ctx")
    tokens_per_shard = queries.shape[0]
    query_heads = QUERY_HEADS // head_count
    heads_per_group = QUERY_HEADS // VALUE_KEY_HEADS
    local_kv = max(1, query_heads // heads_per_group)
    score_scale = HEAD_DIMENSION ** (-0.5)
    placement_index = np.array(
        [
            slot_number * query_heads // heads_per_group + offset
            for slot_number in range(head_count)
            for offset in range(local_kv)
        ],
        dtype=np.int32,
    )
    key_placements = keys.reshape(tokens_per_shard, VALUE_KEY_HEADS, HEAD_DIMENSION)[
        :, placement_index, :
    ].reshape(tokens_per_shard, head_count * local_kv * HEAD_DIMENSION)
    value_placements = values.reshape(tokens_per_shard, VALUE_KEY_HEADS, HEAD_DIMENSION)[
        :, placement_index, :
    ].reshape(tokens_per_shard, head_count * local_kv * HEAD_DIMENSION)
    tok_ctx = tokens_per_shard * head_count
    block_rows = tok_ctx // 2
    query_pos = token_positions(
        block_order, ctx_index * tok_ctx + jnp.arange(tok_ctx, dtype=jnp.int32), block_rows
    )

    def make_fold(query_all, key_heads, position_of):

        def tile(states, key_rows, value_rows, key_pos):
            updated = []
            for number in range(2):
                query_block = query_all[number * block_rows : (number + 1) * block_rows]
                block_pos = query_pos[number * block_rows : (number + 1) * block_rows]
                reach = jnp.min(key_pos) <= jnp.max(block_pos)
                updated.append(
                    lax.cond(
                        reach,
                        lambda carry_state: attend(
                            carry_state,
                            query_block,
                            block_pos,
                            key_rows,
                            value_rows,
                            key_pos,
                            key_heads,
                            score_scale,
                        ),
                        lambda carry_state: carry_state,
                        states[number],
                    )
                )
            return tuple(updated)

        def fold_step(states, key_piece, first_row):
            key_rows, value_rows = key_piece
            count = key_rows.shape[0]
            key_pos = position_of(jnp.arange(count, dtype=jnp.int32))
            piece_rows = tok_ctx * math.gcd(count // tok_ctx, 4)
            splits = count // piece_rows

            def scan_step(carry_states, parts):
                return (tile(carry_states, parts[0], parts[1], parts[2]), None)

            states, unused = lax.scan(
                scan_step,
                states,
                (
                    key_rows.reshape(splits, piece_rows, -1),
                    value_rows.reshape(splits, piece_rows, -1),
                    key_pos.reshape(splits, piece_rows),
                ),
            )
            return states

        return fold_step

    local_q, local_k, local_v = (
        lax.all_to_all(queries, "head", split_axis=1, concat_axis=0, tiled=True),
        lax.all_to_all(key_placements, "head", split_axis=1, concat_axis=0, tiled=True),
        lax.all_to_all(value_placements, "head", split_axis=1, concat_axis=0, tiled=True),
    )

    def full_positions(row_ids):
        return token_positions(block_order, row_ids, block_rows)

    fold_each = make_fold(local_q, local_kv, full_positions)
    one_state = (
        jnp.full((query_heads, block_rows), -1e30, jnp.float32),
        jnp.zeros((query_heads, block_rows), jnp.float32),
        jnp.zeros((block_rows, query_heads * HEAD_DIMENSION), jnp.float32),
    )
    states = fold_each(
        (one_state, one_state),
        (
            lax.all_gather(local_k, "ctx", axis=0, tiled=True),
            lax.all_gather(local_v, "ctx", axis=0, tiled=True),
        ),
        jnp.int32(0),
    )
    total_all = jnp.concatenate([states[0][1], states[1][1]], axis=1)
    weighted_all = jnp.concatenate([states[0][2], states[1][2]], axis=0)
    weighted_all = weighted_all.reshape(tok_ctx, query_heads, HEAD_DIMENSION)
    attended = (
        (weighted_all / total_all.T[:, :, None])
        .reshape(tok_ctx, query_heads * HEAD_DIMENSION)
        .astype(jnp.bfloat16)
    )
    return lax.all_to_all(attended, "head", split_axis=0, concat_axis=1, tiled=True)


ROWS = 20
MAIN = 16
REST = ROWS - MAIN
GROUP = QUERY_HEADS // VALUE_KEY_HEADS
HALF = VALUE_KEY_HEADS * ROWS
ZS = 4
SLOTS = 8 * ZS
Z_ORDER = (1, 3, 2)


def slot_of(core, place, z):
    return (core * 4 + place) * ZS + z


def copy_names():
    names = [("z", r) for r in range(1, ZS)]
    for kind in ("x", "y", "dx", "dy", "m0", "m1", "m2", "mk", "mv"):
        names += [(kind, r) for r in range(ZS)]
    return names


NAMES = copy_names()


def gather_attend(
    block_rows, order_hbm, q_hbm, k_hbm, v_hbm, o_ref,
    order_ref, k_ref, v_ref, q_in, q_all, q_rest, own_rest, chunks, k_rest, v_rest, bias,
    in_sem, send_sem, recv_sem,
):
    ctx, z = lax.axis_index("ctx"), lax.axis_index("head")
    bits = (lax.rem(ctx, 2), lax.rem(lax.div(ctx, 2), 2), lax.div(ctx, 4))
    mate = (ctx + 1 - 2 * bits[0], z)
    x_next = (ctx + 2 - 4 * bits[1], z)
    y_next = (ctx + 4 - 8 * bits[2], z)
    z_to = {r: (ctx, lax.rem(z + ZS - r, ZS)) for r in range(1, ZS)}

    loads = [
        pltpu.make_async_copy(source, sink, in_sem.at[number])
        for number, (source, sink) in enumerate(
            ((k_hbm, k_ref), (v_hbm, v_ref), (order_hbm, order_ref), (q_hbm, q_in))
        )
    ]
    for load in loads:
        load.start()

    barrier = pltpu.get_barrier_semaphore()
    partners = [mate, x_next, y_next] + [z_to[r] for r in range(1, ZS)]
    for partner in partners:
        pl.semaphore_signal(
            barrier, inc=1, device_id=partner, device_id_type=pl.DeviceIdType.MESH
        )

    for which, ref in enumerate((k_ref, v_ref)):
        loads[which].wait()
        base = which * HALF
        for h in range(VALUE_KEY_HEADS):
            lanes = slice(h * HEAD_DIMENSION, (h + 1) * HEAD_DIMENSION)
            chunks[0, base + h * MAIN : base + (h + 1) * MAIN, :] = ref[0:MAIN, lanes]
            own_rest[which, h * REST : (h + 1) * REST, :] = ref[MAIN:ROWS, lanes].astype(
                jnp.float32
            )
        chunks[0, base + VALUE_KEY_HEADS * MAIN : base + HALF, :] = own_rest[which].astype(
            jnp.bfloat16
        )

    ids = {name: number for number, name in enumerate(NAMES)}

    def part(slot, half):
        if half is None:
            return chunks.at[slot]
        return chunks.at[slot, half * HALF : (half + 1) * HALF]

    def copy(name):
        kind, r = name
        target, source, sink, half = {
            "z": (z_to.get(r), slot_of(0, 0, 0), slot_of(0, 0, r), None),
            "x": (x_next, slot_of(0, 0, r), slot_of(0, 1, r), None),
            "y": (y_next, slot_of(0, 0, r), slot_of(0, 2, r), None),
            "dx": (x_next, slot_of(0, 2, r), slot_of(0, 3, r), 1),
            "dy": (y_next, slot_of(0, 1, r), slot_of(0, 3, r), 0),
            "m0": (mate, slot_of(0, 0, r), slot_of(1, 0, r), None),
            "m1": (mate, slot_of(0, 1, r), slot_of(1, 1, r), None),
            "m2": (mate, slot_of(0, 2, r), slot_of(1, 2, r), None),
            "mk": (mate, slot_of(0, 3, r), slot_of(1, 3, r), 0),
            "mv": (mate, slot_of(0, 3, r), slot_of(1, 3, r), 1),
        }[kind]
        return pltpu.make_async_remote_copy(
            src_ref=part(source, half),
            dst_ref=part(sink, half),
            send_sem=send_sem.at[ids[name]],
            recv_sem=recv_sem.at[ids[name]],
            device_id=target,
            device_id_type=pl.DeviceIdType.MESH,
        )

    copies = {name: copy(name) for name in NAMES}

    def rest_rows(slot):
        for which, sink in ((0, k_rest), (1, v_rest)):
            top = which * HALF + VALUE_KEY_HEADS * MAIN
            rows = chunks[slot, top : top + VALUE_KEY_HEADS * REST, :].astype(jnp.float32)
            for h in range(VALUE_KEY_HEADS):
                sink[h, slot * REST : (slot + 1) * REST, :] = rows[h * REST : (h + 1) * REST]

    def arrived(*name):
        copies[name].wait_recv()

    def start(*name):
        copies[name].start()

    pl.semaphore_wait(barrier, len(partners))
    for r in Z_ORDER:
        start("z", r)
    start("x", 0)
    start("y", 0)
    start("m0", 0)

    loads[2].wait()
    lane = lax.broadcasted_iota(jnp.int32, (8, SLOTS * ROWS), 1)
    late = lane >= SLOTS * MAIN
    lane_slot = jnp.where(late, lax.div(lane - SLOTS * MAIN, REST), lax.div(lane, MAIN))
    lane_token = jnp.where(late, MAIN + lax.rem(lane, REST), lax.rem(lane, MAIN))
    key_pos = lane_token

    def first_position(flips, r):
        other = 0
        for number, flip in enumerate(flips):
            bit = 1 - bits[number] if flip else bits[number]
            other = other + bit * (1 << number)
        row = (other * ZS + lax.rem(z + r, ZS)) * ROWS
        return order_ref[lax.div(row, block_rows)] * block_rows + lax.rem(row, block_rows)

    for core in range(2):
        for place in range(4):
            for r in range(ZS):
                at = first_position((core, place % 2, place // 2), r)
                key_pos = key_pos + jnp.where(lane_slot == slot_of(core, place, r), at, 0)
    row = lax.broadcasted_iota(jnp.int32, (HALF, SLOTS * ROWS), 0)
    row_token = jnp.where(row >= GROUP * MAIN, MAIN + lax.rem(row, REST), lax.rem(row, MAIN))
    visible = key_pos[0:1, :] - first_position((0, 0, 0), 0) <= row_token
    bias[...] = jnp.where(visible, 0.0, -jnp.inf)

    loads[3].wait()
    for h in range(VALUE_KEY_HEADS):
        for g in range(GROUP):
            lanes = slice((h * GROUP + g) * HEAD_DIMENSION, (h * GROUP + g + 1) * HEAD_DIMENSION)
            q_all[h, g * MAIN : (g + 1) * MAIN, :] = q_in[0:MAIN, lanes]
            q_rest[h, g * REST : (g + 1) * REST, :] = q_in[MAIN:ROWS, lanes].astype(jnp.float32)
        q_all[h, GROUP * MAIN : HALF, :] = q_rest[h].astype(jnp.bfloat16)
    rest_rows(0)

    def pass_first(r):
        arrived("z", r)
        start("x", r)
        start("y", r)
        start("m0", r)
        rest_rows(slot_of(0, 0, r))

    def pass_second(r):
        arrived("x", r)
        start("dy", r)
        start("m1", r)
        arrived("y", r)
        start("dx", r)
        start("m2", r)
        rest_rows(slot_of(0, 1, r))
        rest_rows(slot_of(0, 2, r))

    def pass_third(r):
        arrived("dy", r)
        start("mk", r)
        arrived("dx", r)
        start("mv", r)
        rest_rows(slot_of(0, 3, r))
        for place in range(3):
            arrived("m%d" % place, r)
            rest_rows(slot_of(1, place, r))

    pass_second(0)
    for r in Z_ORDER:
        pass_first(r)
    pass_third(0)
    for r in Z_ORDER:
        pass_second(r)
    for r in Z_ORDER:
        pass_third(r)
    for r in (0,) + Z_ORDER:
        arrived("mk", r)
        arrived("mv", r)
        rest_rows(slot_of(1, 3, r))

    scale = HEAD_DIMENSION ** (-0.5)
    whole = (((1,), (1,)), ((), ()))
    for h in range(VALUE_KEY_HEADS):
        rows = slice(h * MAIN, (h + 1) * MAIN)
        queries = q_all[h]
        keys = chunks[:, rows, :].reshape(SLOTS * MAIN, HEAD_DIMENSION)
        values = chunks[:, HALF + h * MAIN : HALF + (h + 1) * MAIN, :].reshape(
            SLOTS * MAIN, HEAD_DIMENSION
        )
        scores = jnp.concatenate(
            [
                lax.dot_general(queries, keys, whole, preferred_element_type=jnp.float32),
                lax.dot_general(
                    queries,
                    k_rest[h].astype(jnp.bfloat16),
                    whole,
                    preferred_element_type=jnp.float32,
                ),
            ],
            axis=1,
        ) + bias[...]
        top = jnp.max(scores, axis=1, keepdims=True)
        weights = jnp.exp((scores - top) * scale)
        total = jnp.sum(weights, axis=1, keepdims=True)
        weights = weights.astype(jnp.bfloat16)
        mixed = jnp.dot(
            weights[:, : SLOTS * MAIN], values, preferred_element_type=jnp.float32
        ) + jnp.dot(
            weights[:, SLOTS * MAIN :],
            v_rest[h].astype(jnp.bfloat16),
            preferred_element_type=jnp.float32,
        )
        mixed = mixed / total
        for g in range(GROUP):
            lanes = slice((h * GROUP + g) * HEAD_DIMENSION, (h * GROUP + g + 1) * HEAD_DIMENSION)
            o_ref[0:MAIN, lanes] = mixed[g * MAIN : (g + 1) * MAIN].astype(jnp.bfloat16)
            first = GROUP * MAIN + g * REST
            o_ref[MAIN:ROWS, lanes] = mixed[first : first + REST].astype(jnp.bfloat16)

    for name in NAMES:
        copies[name].wait_send()


def on_device_gathered(queries, keys, values, block_order):
    block_rows = queries.shape[0] * lax.axis_size("ctx") * lax.axis_size("head")
    block_rows = block_rows // block_order.shape[0]
    bf16, f32 = jnp.bfloat16, jnp.float32
    in_hbm = pl.BlockSpec(memory_space=pltpu.HBM)
    return pl.pallas_call(
        functools.partial(gather_attend, block_rows),
        out_shape=jax.ShapeDtypeStruct(queries.shape, bf16),
        in_specs=[in_hbm] * 4,
        out_specs=pl.BlockSpec(memory_space=pltpu.VMEM),
        scratch_shapes=[
            pltpu.SMEM(block_order.shape, jnp.int32),
            pltpu.VMEM(keys.shape, bf16),
            pltpu.VMEM(values.shape, bf16),
            pltpu.VMEM(queries.shape, bf16),
            pltpu.VMEM((VALUE_KEY_HEADS, HALF, HEAD_DIMENSION), bf16),
            pltpu.VMEM((VALUE_KEY_HEADS, GROUP * REST, HEAD_DIMENSION), f32),
            pltpu.VMEM((2, VALUE_KEY_HEADS * REST, HEAD_DIMENSION), f32),
            pltpu.VMEM((SLOTS, 2 * HALF, HEAD_DIMENSION), bf16),
            pltpu.VMEM((VALUE_KEY_HEADS, SLOTS * REST, HEAD_DIMENSION), f32),
            pltpu.VMEM((VALUE_KEY_HEADS, SLOTS * REST, HEAD_DIMENSION), f32),
            pltpu.VMEM((HALF, SLOTS * ROWS), f32),
            pltpu.SemaphoreType.DMA((4,)),
            pltpu.SemaphoreType.DMA((len(NAMES),)),
            pltpu.SemaphoreType.DMA((len(NAMES),)),
        ],
        compiler_params=pltpu.CompilerParams(
            collective_id=0, has_side_effects=True, vmem_limit_bytes=60 * 1024 * 1024
        ),
    )(block_order, queries, keys, values)


def gathers_whole(mesh, queries, block_order):
    if mesh.shape["ctx"] != 8 or mesh.shape["head"] != ZS:
        return False
    rows = queries.shape[0]
    return rows == SLOTS * ROWS and (rows // block_order.shape[0]) % ROWS == 0


def solution(mesh):
    placed = (P(("ctx", "head"), None), P(("ctx", "head"), None), P(("ctx", "head"), None), P())

    def run(queries, keys, values, block_order):
        body = on_device_gathered if gathers_whole(mesh, queries, block_order) else on_device
        return jax.shard_map(
            body, mesh=mesh, in_specs=placed, out_specs=P(("ctx", "head"), None), check_vma=False
        )(queries, keys, values, block_order)

    return run
```

```python
import functools
import math

import jax
import jax.numpy as jnp
import numpy as np
from jax import lax
from jax.experimental import pallas as pl
from jax.experimental.pallas import tpu as pltpu
from jax.sharding import PartitionSpec as P

QUERY_HEADS = 64
VALUE_KEY_HEADS = 8
HEAD_DIMENSION = 128


def token_positions(block_order, row_ids, block_rows):
    block_ids = row_ids // block_rows
    block_table = jnp.arange(block_order.shape[0], dtype=jnp.int32)
    chosen = jnp.sum(
        jnp.where(block_ids[:, None] == block_table[None, :], block_order[None, :], 0), axis=1
    )
    return chosen * block_rows + row_ids % block_rows


def attend(states, query_block, query_pos, key_rows, value_rows, key_pos, key_heads, score_scale):
    max_old, total_old, weighted_old = states
    query_count = query_block.shape[0]
    head_size = key_rows.shape[1] // key_heads
    heads_per_group = query_block.shape[1] // (key_heads * head_size)
    head_total = key_heads * heads_per_group
    query_split = query_block.reshape(query_count, key_heads, heads_per_group, head_size)
    key_split = key_rows.reshape(-1, key_heads, head_size)
    value_split = value_rows.reshape(-1, key_heads, head_size)
    scores = (
        jnp.einsum("qkgd,nkd->kgqn", query_split, key_split, preferred_element_type=jnp.float32)
        * score_scale
    )
    visible = key_pos[None, :] <= query_pos[:, None]
    scores = jnp.where(visible[None, None], scores, -jnp.inf)
    max_prev = max_old.reshape(key_heads, heads_per_group, query_count)
    max_new = jnp.maximum(max_prev, jnp.max(scores, axis=3))
    weights = jnp.exp(scores - max_new[..., None])
    rescale = jnp.exp(max_prev - max_new)
    total_new = total_old.reshape(key_heads, heads_per_group, query_count) * rescale + jnp.sum(
        weights, axis=3
    )
    mixed_values = jnp.einsum(
        "kgqn,nkd->qkgd",
        weights.astype(jnp.bfloat16),
        value_split,
        preferred_element_type=jnp.float32,
    )
    weighted_new = (
        weighted_old.reshape(query_count, key_heads, heads_per_group, head_size)
        * jnp.transpose(rescale, (2, 0, 1))[..., None]
        + mixed_values
    )
    return (
        max_new.reshape(head_total, query_count),
        total_new.reshape(head_total, query_count),
        weighted_new.reshape(query_count, head_total * head_size),
    )


def on_device(queries, keys, values, block_order):
    head_count = lax.axis_size("head")
    ctx_index = lax.axis_index("ctx")
    tokens_per_shard = queries.shape[0]
    query_heads = QUERY_HEADS // head_count
    heads_per_group = QUERY_HEADS // VALUE_KEY_HEADS
    local_kv = max(1, query_heads // heads_per_group)
    score_scale = HEAD_DIMENSION ** (-0.5)
    placement_index = np.array(
        [
            slot_number * query_heads // heads_per_group + offset
            for slot_number in range(head_count)
            for offset in range(local_kv)
        ],
        dtype=np.int32,
    )
    key_placements = keys.reshape(tokens_per_shard, VALUE_KEY_HEADS, HEAD_DIMENSION)[
        :, placement_index, :
    ].reshape(tokens_per_shard, head_count * local_kv * HEAD_DIMENSION)
    value_placements = values.reshape(tokens_per_shard, VALUE_KEY_HEADS, HEAD_DIMENSION)[
        :, placement_index, :
    ].reshape(tokens_per_shard, head_count * local_kv * HEAD_DIMENSION)
    tok_ctx = tokens_per_shard * head_count
    block_rows = tok_ctx // 2
    query_pos = token_positions(
        block_order, ctx_index * tok_ctx + jnp.arange(tok_ctx, dtype=jnp.int32), block_rows
    )

    def make_fold(query_all, key_heads, position_of):

        def tile(states, key_rows, value_rows, key_pos):
            updated = []
            for number in range(2):
                query_block = query_all[number * block_rows : (number + 1) * block_rows]
                block_pos = query_pos[number * block_rows : (number + 1) * block_rows]
                reach = jnp.min(key_pos) <= jnp.max(block_pos)
                updated.append(
                    lax.cond(
                        reach,
                        lambda carry_state: attend(
                            carry_state,
                            query_block,
                            block_pos,
                            key_rows,
                            value_rows,
                            key_pos,
                            key_heads,
                            score_scale,
                        ),
                        lambda carry_state: carry_state,
                        states[number],
                    )
                )
            return tuple(updated)

        def fold_step(states, key_piece, first_row):
            key_rows, value_rows = key_piece
            count = key_rows.shape[0]
            key_pos = position_of(jnp.arange(count, dtype=jnp.int32))
            piece_rows = tok_ctx * math.gcd(count // tok_ctx, 4)
            splits = count // piece_rows

            def scan_step(carry_states, parts):
                return (tile(carry_states, parts[0], parts[1], parts[2]), None)

            states, unused = lax.scan(
                scan_step,
                states,
                (
                    key_rows.reshape(splits, piece_rows, -1),
                    value_rows.reshape(splits, piece_rows, -1),
                    key_pos.reshape(splits, piece_rows),
                ),
            )
            return states

        return fold_step

    local_q, local_k, local_v = (
        lax.all_to_all(queries, "head", split_axis=1, concat_axis=0, tiled=True),
        lax.all_to_all(key_placements, "head", split_axis=1, concat_axis=0, tiled=True),
        lax.all_to_all(value_placements, "head", split_axis=1, concat_axis=0, tiled=True),
    )

    def full_positions(row_ids):
        return token_positions(block_order, row_ids, block_rows)

    fold_each = make_fold(local_q, local_kv, full_positions)
    one_state = (
        jnp.full((query_heads, block_rows), -1e30, jnp.float32),
        jnp.zeros((query_heads, block_rows), jnp.float32),
        jnp.zeros((block_rows, query_heads * HEAD_DIMENSION), jnp.float32),
    )
    states = fold_each(
        (one_state, one_state),
        (
            lax.all_gather(local_k, "ctx", axis=0, tiled=True),
            lax.all_gather(local_v, "ctx", axis=0, tiled=True),
        ),
        jnp.int32(0),
    )
    total_all = jnp.concatenate([states[0][1], states[1][1]], axis=1)
    weighted_all = jnp.concatenate([states[0][2], states[1][2]], axis=0)
    weighted_all = weighted_all.reshape(tok_ctx, query_heads, HEAD_DIMENSION)
    attended = (
        (weighted_all / total_all.T[:, :, None])
        .reshape(tok_ctx, query_heads * HEAD_DIMENSION)
        .astype(jnp.bfloat16)
    )
    return lax.all_to_all(attended, "head", split_axis=0, concat_axis=1, tiled=True)


ROWS = 20
MAIN = 16
REST = ROWS - MAIN
GROUP = QUERY_HEADS // VALUE_KEY_HEADS
HALF = VALUE_KEY_HEADS * ROWS
ZS = 4
SLOTS = 8 * ZS
Z_ORDER = (1, 3, 2)
DIRECT = (0, 2)


def slot_of(core, place, z):
    return (core * 4 + place) * ZS + z


def copy_names():
    names = [("z", r) for r in range(1, ZS)]
    for kind in ("x", "y", "dx", "dy", "m0", "m1", "m2", "mk", "mv"):
        names += [(kind, r) for r in range(ZS)]
    return names


NAMES = copy_names()


def gather_attend(
    block_rows, order_hbm, q_hbm, k_hbm, v_hbm, o_ref,
    order_ref, k_ref, v_ref, q_in, q_all, q_rest, own_rest, chunks, k_rest, v_rest, bias,
    in_sem, send_sem, recv_sem,
):
    ctx, z = lax.axis_index("ctx"), lax.axis_index("head")
    bits = (lax.rem(ctx, 2), lax.rem(lax.div(ctx, 2), 2), lax.div(ctx, 4))
    mate = (ctx + 1 - 2 * bits[0], z)
    x_next = (ctx + 2 - 4 * bits[1], z)
    y_next = (ctx + 4 - 8 * bits[2], z)
    across = (ctx + 6 - 4 * bits[1] - 8 * bits[2], z)
    z_to = {r: (ctx, lax.rem(z + ZS - r, ZS)) for r in range(1, ZS)}

    loads = [
        pltpu.make_async_copy(source, sink, in_sem.at[number])
        for number, (source, sink) in enumerate(
            ((k_hbm, k_ref), (v_hbm, v_ref), (order_hbm, order_ref), (q_hbm, q_in))
        )
    ]
    for load in loads:
        load.start()

    barrier = pltpu.get_barrier_semaphore()
    partners = [mate, x_next, y_next, across] + [z_to[r] for r in range(1, ZS)]
    for partner in partners:
        pl.semaphore_signal(
            barrier, inc=1, device_id=partner, device_id_type=pl.DeviceIdType.MESH
        )

    for which, ref in enumerate((k_ref, v_ref)):
        loads[which].wait()
        base = which * HALF
        for h in range(VALUE_KEY_HEADS):
            lanes = slice(h * HEAD_DIMENSION, (h + 1) * HEAD_DIMENSION)
            chunks[0, base + h * MAIN : base + (h + 1) * MAIN, :] = ref[0:MAIN, lanes]
            own_rest[which, h * REST : (h + 1) * REST, :] = ref[MAIN:ROWS, lanes].astype(
                jnp.float32
            )
        chunks[0, base + VALUE_KEY_HEADS * MAIN : base + HALF, :] = own_rest[which].astype(
            jnp.bfloat16
        )

    ids = {name: number for number, name in enumerate(NAMES)}

    def part(slot, half):
        if half is None:
            return chunks.at[slot]
        return chunks.at[slot, half * HALF : (half + 1) * HALF]

    def copy(name):
        kind, r = name
        direct = r in DIRECT
        target, source, sink, half = {
            "z": (z_to.get(r), slot_of(0, 0, 0), slot_of(0, 0, r), None),
            "x": (x_next, slot_of(0, 0, r), slot_of(0, 1, r), None),
            "y": (y_next, slot_of(0, 0, r), slot_of(0, 2, r), None),
            "dx": (across if direct else x_next, slot_of(0, 0 if direct else 2, r), slot_of(0, 3, r), 1),
            "dy": (across if direct else y_next, slot_of(0, 0 if direct else 1, r), slot_of(0, 3, r), 0),
            "m0": (mate, slot_of(0, 0, r), slot_of(1, 0, r), None),
            "m1": (mate, slot_of(0, 1, r), slot_of(1, 1, r), None),
            "m2": (mate, slot_of(0, 2, r), slot_of(1, 2, r), None),
            "mk": (mate, slot_of(0, 3, r), slot_of(1, 3, r), 0),
            "mv": (mate, slot_of(0, 3, r), slot_of(1, 3, r), 1),
        }[kind]
        return pltpu.make_async_remote_copy(
            src_ref=part(source, half),
            dst_ref=part(sink, half),
            send_sem=send_sem.at[ids[name]],
            recv_sem=recv_sem.at[ids[name]],
            device_id=target,
            device_id_type=pl.DeviceIdType.MESH,
        )

    copies = {name: copy(name) for name in NAMES}

    def rest_rows(slot):
        for which, sink in ((0, k_rest), (1, v_rest)):
            top = which * HALF + VALUE_KEY_HEADS * MAIN
            rows = chunks[slot, top : top + VALUE_KEY_HEADS * REST, :].astype(jnp.float32)
            for h in range(VALUE_KEY_HEADS):
                sink[h, slot * REST : (slot + 1) * REST, :] = rows[h * REST : (h + 1) * REST]

    def arrived(*name):
        copies[name].wait_recv()

    def start(*name):
        copies[name].start()

    pl.semaphore_wait(barrier, len(partners))
    for r in Z_ORDER:
        start("z", r)
    start("x", 0)
    start("y", 0)
    start("m0", 0)
    if 0 in DIRECT:
        start("dy", 0)
        start("dx", 0)

    loads[2].wait()
    lane = lax.broadcasted_iota(jnp.int32, (8, SLOTS * ROWS), 1)
    late = lane >= SLOTS * MAIN
    lane_slot = jnp.where(late, lax.div(lane - SLOTS * MAIN, REST), lax.div(lane, MAIN))
    lane_token = jnp.where(late, MAIN + lax.rem(lane, REST), lax.rem(lane, MAIN))
    key_pos = lane_token

    def first_position(flips, r):
        other = 0
        for number, flip in enumerate(flips):
            bit = 1 - bits[number] if flip else bits[number]
            other = other + bit * (1 << number)
        row = (other * ZS + lax.rem(z + r, ZS)) * ROWS
        return order_ref[lax.div(row, block_rows)] * block_rows + lax.rem(row, block_rows)

    for core in range(2):
        for place in range(4):
            for r in range(ZS):
                at = first_position((core, place % 2, place // 2), r)
                key_pos = key_pos + jnp.where(lane_slot == slot_of(core, place, r), at, 0)
    row = lax.broadcasted_iota(jnp.int32, (HALF, SLOTS * ROWS), 0)
    row_token = jnp.where(row >= GROUP * MAIN, MAIN + lax.rem(row, REST), lax.rem(row, MAIN))
    visible = key_pos[0:1, :] - first_position((0, 0, 0), 0) <= row_token
    bias[...] = jnp.where(visible, 0.0, -jnp.inf)

    loads[3].wait()
    for h in range(VALUE_KEY_HEADS):
        for g in range(GROUP):
            lanes = slice((h * GROUP + g) * HEAD_DIMENSION, (h * GROUP + g + 1) * HEAD_DIMENSION)
            q_all[h, g * MAIN : (g + 1) * MAIN, :] = q_in[0:MAIN, lanes]
            q_rest[h, g * REST : (g + 1) * REST, :] = q_in[MAIN:ROWS, lanes].astype(jnp.float32)
        q_all[h, GROUP * MAIN : HALF, :] = q_rest[h].astype(jnp.bfloat16)
    rest_rows(0)

    def pass_first(r):
        arrived("z", r)
        start("x", r)
        start("y", r)
        start("m0", r)
        if r in DIRECT:
            start("dy", r)
            start("dx", r)
        rest_rows(slot_of(0, 0, r))

    def pass_second(r):
        arrived("x", r)
        if r not in DIRECT:
            start("dy", r)
        start("m1", r)
        arrived("y", r)
        if r not in DIRECT:
            start("dx", r)
        start("m2", r)
        rest_rows(slot_of(0, 1, r))
        rest_rows(slot_of(0, 2, r))

    def pass_third(r):
        arrived("dy", r)
        start("mk", r)
        arrived("dx", r)
        start("mv", r)
        rest_rows(slot_of(0, 3, r))
        for place in range(3):
            arrived("m%d" % place, r)
            rest_rows(slot_of(1, place, r))

    pass_second(0)
    for r in Z_ORDER:
        pass_first(r)
    pass_third(0)
    for r in Z_ORDER:
        pass_second(r)
    for r in Z_ORDER:
        pass_third(r)
    for r in (0,) + Z_ORDER:
        arrived("mk", r)
        arrived("mv", r)
        rest_rows(slot_of(1, 3, r))

    scale = HEAD_DIMENSION ** (-0.5)
    whole = (((1,), (1,)), ((), ()))
    for h in range(VALUE_KEY_HEADS):
        rows = slice(h * MAIN, (h + 1) * MAIN)
        queries = q_all[h]
        keys = chunks[:, rows, :].reshape(SLOTS * MAIN, HEAD_DIMENSION)
        values = chunks[:, HALF + h * MAIN : HALF + (h + 1) * MAIN, :].reshape(
            SLOTS * MAIN, HEAD_DIMENSION
        )
        scores = jnp.concatenate(
            [
                lax.dot_general(queries, keys, whole, preferred_element_type=jnp.float32),
                lax.dot_general(
                    queries,
                    k_rest[h].astype(jnp.bfloat16),
                    whole,
                    preferred_element_type=jnp.float32,
                ),
            ],
            axis=1,
        ) + bias[...]
        top = jnp.max(scores, axis=1, keepdims=True)
        weights = jnp.exp((scores - top) * scale)
        total = jnp.sum(weights, axis=1, keepdims=True)
        weights = weights.astype(jnp.bfloat16)
        mixed = jnp.dot(
            weights[:, : SLOTS * MAIN], values, preferred_element_type=jnp.float32
        ) + jnp.dot(
            weights[:, SLOTS * MAIN :],
            v_rest[h].astype(jnp.bfloat16),
            preferred_element_type=jnp.float32,
        )
        mixed = mixed / total
        for g in range(GROUP):
            lanes = slice((h * GROUP + g) * HEAD_DIMENSION, (h * GROUP + g + 1) * HEAD_DIMENSION)
            o_ref[0:MAIN, lanes] = mixed[g * MAIN : (g + 1) * MAIN].astype(jnp.bfloat16)
            first = GROUP * MAIN + g * REST
            o_ref[MAIN:ROWS, lanes] = mixed[first : first + REST].astype(jnp.bfloat16)

    for name in NAMES:
        copies[name].wait_send()


def on_device_gathered(queries, keys, values, block_order):
    block_rows = queries.shape[0] * lax.axis_size("ctx") * lax.axis_size("head")
    block_rows = block_rows // block_order.shape[0]
    bf16, f32 = jnp.bfloat16, jnp.float32
    in_hbm = pl.BlockSpec(memory_space=pltpu.HBM)
    return pl.pallas_call(
        functools.partial(gather_attend, block_rows),
        out_shape=jax.ShapeDtypeStruct(queries.shape, bf16),
        in_specs=[in_hbm] * 4,
        out_specs=pl.BlockSpec(memory_space=pltpu.VMEM),
        scratch_shapes=[
            pltpu.SMEM(block_order.shape, jnp.int32),
            pltpu.VMEM(keys.shape, bf16),
            pltpu.VMEM(values.shape, bf16),
            pltpu.VMEM(queries.shape, bf16),
            pltpu.VMEM((VALUE_KEY_HEADS, HALF, HEAD_DIMENSION), bf16),
            pltpu.VMEM((VALUE_KEY_HEADS, GROUP * REST, HEAD_DIMENSION), f32),
            pltpu.VMEM((2, VALUE_KEY_HEADS * REST, HEAD_DIMENSION), f32),
            pltpu.VMEM((SLOTS, 2 * HALF, HEAD_DIMENSION), bf16),
            pltpu.VMEM((VALUE_KEY_HEADS, SLOTS * REST, HEAD_DIMENSION), f32),
            pltpu.VMEM((VALUE_KEY_HEADS, SLOTS * REST, HEAD_DIMENSION), f32),
            pltpu.VMEM((HALF, SLOTS * ROWS), f32),
            pltpu.SemaphoreType.DMA((4,)),
            pltpu.SemaphoreType.DMA((len(NAMES),)),
            pltpu.SemaphoreType.DMA((len(NAMES),)),
        ],
        compiler_params=pltpu.CompilerParams(
            collective_id=0, has_side_effects=True, vmem_limit_bytes=60 * 1024 * 1024
        ),
    )(block_order, queries, keys, values)


def gathers_whole(mesh, queries, block_order):
    if mesh.shape["ctx"] != 8 or mesh.shape["head"] != ZS:
        return False
    rows = queries.shape[0]
    return rows == SLOTS * ROWS and (rows // block_order.shape[0]) % ROWS == 0


def solution(mesh):
    placed = (P(("ctx", "head"), None), P(("ctx", "head"), None), P(("ctx", "head"), None), P())

    def run(queries, keys, values, block_order):
        body = on_device_gathered if gathers_whole(mesh, queries, block_order) else on_device
        return jax.shard_map(
            body, mesh=mesh, in_specs=placed, out_specs=P(("ctx", "head"), None), check_vma=False
        )(queries, keys, values, block_order)

    return run
```
